256 devices in a mesh: state: 8 (over z_lo, y), snap: 32 (over x, z_hi, core).
Axes of the slice: x: 4, y: 4, z: 8 (z_hi: 4, z_lo: 2; z = z_hi * 2 + z_lo), core: 2. Of those that a mesh axis runs over, the one named last changes fastest.
Arguments:
- snapshots: bfloat16 [1024, 393216], P('snap', 'state'), may hold values from -64 to 64
- coefficients: bfloat16 [1024, 128], replicated, may hold values from -0.1875 to 0.1875
Outputs:
- gram: float32 [1024, 1024], P('snap', 'state')
- modes: float32 [393216, 128], P(('state', 'snap'))
The draws below stay inside these ranges and needn't reach their ends.
All inputs are finite; a program needn't handle non-finite values.
Results may differ from the reference program's by a relative error of at most 0.0003.
Values may be sent and summed in bfloat16 or wider, within the bound.
No kernel may reach another device: no remote copies, remote signals or barrier semaphores. Data moves between devices by JAX's collectives and lax.ppermute only.
A program may use at most 64 MiB of HBM per device.

```python
import jax
import jax.numpy as jnp
from jax import lax

NS = 1024
K = 128
ROWS = 393216


def draw_snapshots(key, part):
    key = jax.random.fold_in(key, 7)
    key_noise, key_rows, key_cols = jax.random.split(key, 3)
    place = jnp.arange(ROWS, dtype=jnp.float32)[None, :] / ROWS
    row_scale = 0.3 * 10.0 ** (0.5 * place + 0.5 * jax.random.uniform(key_rows, (1, ROWS), jnp.float32))
    col_scale = 0.3 * 10.0 ** jax.random.uniform(key_cols, (NS, 1), jnp.float32)
    noise = jax.random.truncated_normal(key_noise, -4.0, 4.0, (NS, ROWS), jnp.float32)
    values = row_scale * col_scale * noise
    return values.astype(jnp.bfloat16)


def scatter_about(stream_key, dims, deviation, most, kind=jnp.bfloat16):
    entries = jax.random.normal(stream_key, dims, jnp.float32) * deviation
    return jnp.minimum(jnp.maximum(entries, -most), most).astype(kind)


def setup_inputs(seed: int = 0) -> dict:
    splits = jax.random.split(jax.random.key(seed), 3)
    return {
        "snapshots": draw_snapshots(jax.random.fold_in(splits[2], 71), 0),
        "coefficients": scatter_about(splits[1], (NS, K), NS ** -0.5, 0.1875),
    }


def reference(snapshots, coefficients):
    full_gram = lax.dot_general(snapshots, snapshots, (((1,), (1,)), ((), ())), preferred_element_type=jnp.float32)
    gram = full_gram / ROWS
    weights = coefficients.astype(jnp.float32)
    energy = lax.optimization_barrier(jnp.sum(jnp.dot(full_gram, weights, precision=lax.Precision.HIGHEST) * weights, axis=0))
    raw = lax.dot_general(snapshots, coefficients, (((0,), (0,)), ((), ())), preferred_element_type=jnp.float32)
    modes = raw * lax.rsqrt(energy / ROWS + 1e-06)
    return (gram, modes)
```

```python
import jax
import jax.numpy as jnp
from jax import lax
from jax.sharding import Mesh, PartitionSpec as P

NS = 1024
PLANE = ("zlo", "y", "x")
SNAP = ("x", "zhi", "core")
STATE = ("zlo", "y")


def body(snapshots, coefficients):
    width, count = snapshots.shape
    parts = lax.axis_size(SNAP)
    stripes = lax.axis_size(STATE)
    nx, nz, nc = (lax.axis_size(a) for a in SNAP)
    group = stripes * nx
    col = NS // stripes
    all_rows = count * stripes
    core = lax.axis_index("core")
    row_block = lax.all_to_all(snapshots, SNAP, split_axis=1, concat_axis=0, tiled=True)
    raw = lax.dot_general(
        row_block, coefficients, (((0,), (0,)), ((), ())), preferred_element_type=jnp.float32
    )
    energy = jnp.sum(raw * raw, axis=0)
    left = row_block.reshape(nx, nz, nc, width, -1)
    right = row_block.reshape(stripes, col, -1)
    gram = jnp.einsum("xzkrn,scn->ksxzrc", left, right, preferred_element_type=jnp.float32)
    gram = gram.reshape(nc, group, nz * width, col)
    mine = lax.dynamic_index_in_dim(gram, core, 0, keepdims=False)
    other = lax.dynamic_index_in_dim(gram, 1 - core, 0, keepdims=False)
    swap = [(i, 1 - i) for i in range(nc)]
    got = lax.ppermute(other, "core", swap)
    energy = energy + lax.ppermute(energy, "core", swap)
    half = mine + got
    tail = jnp.broadcast_to(energy[None, None, :], (group, 8, col))
    sent = jnp.concatenate([half, tail], axis=1)
    plane = jnp.sum(lax.all_to_all(sent, PLANE, 0, 0, tiled=True), axis=0)
    quarter = plane[: nz * width].reshape(nz, width, col)
    tail = jnp.broadcast_to(plane[None, nz * width :], (nz, 8, col))
    sent = jnp.concatenate([quarter, tail], axis=1)
    total = jnp.sum(lax.all_to_all(sent, "zhi", 0, 0, tiled=True), axis=0)
    gram = total[:width] / all_rows
    modes = raw * lax.rsqrt(total[width] / all_rows + 1e-06)
    return (gram, modes)


def solution(mesh):
    fine = Mesh(mesh.devices.reshape(2, 4, 4, 4, 2), ("zlo", "y", "x", "zhi", "core"))
    return jax.shard_map(
        body,
        mesh=fine,
        in_specs=(P(SNAP, STATE), P()),
        out_specs=(P(SNAP, STATE), P(STATE + SNAP, None)),
        check_vma=False,
    )
```

```python
import functools

import jax
import jax.numpy as jnp
from jax import lax
from jax.experimental import pallas as pl
from jax.experimental.pallas import tpu as pltpu
from jax.sharding import Mesh, PartitionSpec as P

ALL = ("zlo", "y", "x", "zhi", "core")
PLANE = ("zlo", "y", "x")
SNAP = ("x", "zhi", "core")
STATE = ("zlo", "y")
B = 128
NB = 8
W = 32
HALF = 40
CHUNK = 2 * HALF
PAIR = 2 * B
F32 = jnp.float32


def block(a, s):
    return s * (s + 1) // 2 + a


BLOCKS = NB * (NB + 1) // 2


def gram_kernel(core_ref, rows_ref, coef_ref, mine_ref, other_ref, raw_ref, tile_ref):
    core = core_ref[0]
    raw_t = lax.dot_general(
        coef_ref[...], rows_ref[...], (((0,), (0,)), ((), ())), preferred_element_type=F32
    )
    raw = raw_t.T
    raw_ref[...] = raw
    energy = jnp.broadcast_to(jnp.sum(raw * raw, axis=0, keepdims=True), (W, B))
    mine_ref[pl.ds(BLOCKS, W, stride=CHUNK), :] = energy
    other_ref[pl.ds(BLOCKS, W, stride=CHUNK), :] = energy
    for sp in range(NB // 2):
        depth = (sp + 1) * PAIR
        tile_ref[:depth, :] = lax.dot_general(
            rows_ref[:depth, :],
            rows_ref[sp * PAIR : (sp + 1) * PAIR, :],
            (((1,), (1,)), ((), ())),
            preferred_element_type=F32,
        )
        for t in range(2):
            s = 2 * sp + t
            for a in range(s + 1):
                for slot in range(2):
                    top = a * B + slot * 2 * W
                    row = slot * HALF + block(a, s)
                    for out_ref, c in ((mine_ref, core), (other_ref, 1 - core)):
                        out_ref[pl.ds(row, W, stride=CHUNK), :] = tile_ref[
                            pl.ds(pl.multiple_of(top + c * W, W), W), t * B : (t + 1) * B
                        ]


def spread_kernel(core_ref, got_ref, out_ref, direct_ref, turned_ref):
    core = core_ref[0]
    total = got_ref[0]
    for i in range(1, W):
        total = total + got_ref[i]
    u = (total[:HALF], total[HALF:])
    energy = total[BLOCKS : BLOCKS + 1]
    lane = lax.broadcasted_iota(jnp.int32, (HALF, B), 1)
    part = jnp.where(core == 0, pltpu.roll(energy, B // 2, 1), energy)
    part = jnp.broadcast_to(part, (HALF, B))
    whole = jnp.broadcast_to(energy, (HALF, B))
    for q in range(B // W):
        direct_ref[q] = jnp.where(core == q % 2, u[q // 2], whole)
        first = u[0] if q == 0 else pltpu.roll(u[0], B - W * q, 1)
        second = u[1] if q == 1 else pltpu.roll(u[1], (W - W * q) % B, 1)
        turned_ref[q] = jnp.where(lane < W, first, jnp.where(lane < 2 * W, second, part))
    for s in range(NB):
        for a in range(NB):
            for q in range(B // W):
                dst = s * W + a * (B // W) + q
                if a <= s:
                    row = direct_ref[q, pl.ds(block(a, s), 1), :]
                else:
                    row = turned_ref[q, pl.ds(block(s, a), 1), :]
                out_ref[pl.ds(dst, 1), :] = row


def finish_kernel(all_rows, nz, flag_ref, got_ref, raw_ref, gram_ref, modes_ref):
    core, straight = flag_ref[0], flag_ref[1]
    sums = []
    for c in range(2):
        total = got_ref[pl.ds(c, W, stride=2 * nz), :]
        for z in range(1, nz):
            total = total + got_ref[pl.ds(2 * z + c, W, stride=2 * nz), :]
        sums.append(total)
    direct = jnp.where(core == 0, sums[0], sums[1])
    whole = jnp.where(core == 0, sums[1], sums[0])[:1]
    turned = jnp.concatenate([sums[0], sums[1], sums[0], sums[1]], axis=0).T
    lane = lax.broadcasted_iota(jnp.int32, (W, B), 1)
    turned = jnp.where(lane < B // 2, turned[:W], turned[W : 2 * W])
    halves = jnp.where(lane[:1] < B // 2, pltpu.roll(sums[0][:1], B // 2, 1), sums[1][:1])
    gram_ref[...] = jnp.where(straight == 1, direct, turned) / all_rows
    energy = jnp.where(straight == 1, whole, halves)
    modes_ref[...] = raw_ref[...] * lax.rsqrt(energy / all_rows + 1e-06)


VMEM = pl.BlockSpec(memory_space=pltpu.VMEM)
SMEM = pl.BlockSpec(memory_space=pltpu.SMEM)


def call(kernel, ins, outs, scratch, flops, moved):
    return pl.pallas_call(
        kernel,
        in_specs=[SMEM] + [VMEM] * ins,
        out_specs=tuple(VMEM for _ in outs),
        out_shape=tuple(jax.ShapeDtypeStruct(shape, F32) for shape in outs),
        scratch_shapes=[pltpu.VMEM(shape, F32) for shape in scratch],
        compiler_params=pltpu.CompilerParams(vmem_limit_bytes=40 << 20),
        cost_estimate=pl.CostEstimate(flops=flops, bytes_accessed=moved, transcendentals=0),
    )


def body(snapshots, coefficients):
    count = snapshots.shape[1]
    nz, nc = lax.axis_size("zhi"), lax.axis_size("core")
    all_rows = count * lax.axis_size(STATE)
    devices = lax.axis_size(ALL)
    core = lax.axis_index("core").astype(jnp.int32)
    own_row = lax.axis_index(SNAP) * W // B
    straight = (own_row <= lax.axis_index(STATE)).astype(jnp.int32)
    rows = lax.all_to_all(snapshots, SNAP, split_axis=1, concat_axis=0, tiled=True)
    n = rows.shape[1]
    ns = rows.shape[0]
    mine, other, raw = call(
        gram_kernel,
        2,
        [(W * CHUNK, B), (W * CHUNK, B), (n, B)],
        [(ns, PAIR)],
        2 * ns * n * (5 * ns // 8 + B),
        2 * ns * n + 8 * W * CHUNK * B + 4 * n * B,
    )(core[None], rows, coefficients)
    swap = [(i, 1 - i) for i in range(nc)]
    half = mine + lax.ppermute(other, "core", swap)
    got = lax.all_to_all(half.reshape(W, CHUNK, B), PLANE, 0, 0, tiled=True)
    (spread,) = call(
        spread_kernel, 1, [(devices, B)], [(B // W, HALF, B)] * 2, W * CHUNK * B, 4 * W * CHUNK * B
    )(core[None], got)
    got = lax.all_to_all(spread.reshape(devices, 1, B), ALL, 0, 0, tiled=True)
    gram, modes = call(
        functools.partial(finish_kernel, all_rows, nz),
        2,
        [(W, B), (n, B)],
        [],
        n * B,
        8 * n * B,
    )(jnp.stack([core, straight]), got.reshape(devices, B), raw)
    return (gram, modes)


def solution(mesh):
    fine = Mesh(mesh.devices.reshape(2, 4, 4, 4, 2), ALL)
    return jax.shard_map(
        body,
        mesh=fine,
        in_specs=(P(SNAP, STATE), P()),
        out_specs=(P(SNAP, STATE), P(STATE + SNAP, None)),
        check_vma=False,
    )
```

```python
import functools

import jax
import jax.numpy as jnp
from jax import lax
from jax.experimental import pallas as pl
from jax.experimental.pallas import tpu as pltpu
from jax.sharding import Mesh, PartitionSpec as P

ALL = ("zlo", "y", "x", "zhi", "core")
PLANE = ("zlo", "y", "x")
SNAP = ("x", "zhi", "core")
STATE = ("zlo", "y")
B = 128
NB = 8
W = 32
HALF = 40
CHUNK = 2 * HALF
PAIR = 2 * B
F32 = jnp.float32


def block(a, s):
    return s * (s + 1) // 2 + a


BLOCKS = NB * (NB + 1) // 2


def gram_kernel(rows_ref, coef_ref, mine_ref, other_ref, raw_ref, tile_ref):
    core = lax.axis_index("core")
    raw_t = lax.dot_general(
        coef_ref[...], rows_ref[...], (((0,), (0,)), ((), ())), preferred_element_type=F32
    )
    raw = raw_t.T
    raw_ref[...] = raw
    energy = jnp.broadcast_to(jnp.sum(raw * raw, axis=0, keepdims=True), (W, B))
    mine_ref[pl.ds(BLOCKS, W, stride=CHUNK), :] = energy
    other_ref[pl.ds(BLOCKS, W, stride=CHUNK), :] = energy
    for sp in range(NB // 2):
        depth = (sp + 1) * PAIR
        tile_ref[:depth, :] = lax.dot_general(
            rows_ref[:depth, :],
            rows_ref[sp * PAIR : (sp + 1) * PAIR, :],
            (((1,), (1,)), ((), ())),
            preferred_element_type=F32,
        )
        for t in range(2):
            s = 2 * sp + t
            for a in range(s + 1):
                for slot in range(2):
                    top = a * B + slot * 2 * W
                    row = slot * HALF + block(a, s)
                    for out_ref, c in ((mine_ref, core), (other_ref, 1 - core)):
                        out_ref[pl.ds(row, W, stride=CHUNK), :] = tile_ref[
                            pl.ds(pl.multiple_of(top + c * W, W), W), t * B : (t + 1) * B
                        ]


def spread_kernel(got_ref, out_ref, direct_ref, turned_ref):
    core = lax.axis_index("core")
    total = got_ref[0]
    for i in range(1, W):
        total = total + got_ref[i]
    u = (total[:HALF], total[HALF:])
    energy = total[BLOCKS : BLOCKS + 1]
    lane = lax.broadcasted_iota(jnp.int32, (HALF, B), 1)
    part = jnp.where(core == 0, pltpu.roll(energy, B // 2, 1), energy)
    part = jnp.broadcast_to(part, (HALF, B))
    whole = jnp.broadcast_to(energy, (HALF, B))
    for q in range(B // W):
        direct_ref[q] = jnp.where(core == q % 2, u[q // 2], whole)
        first = u[0] if q == 0 else pltpu.roll(u[0], B - W * q, 1)
        second = u[1] if q == 1 else pltpu.roll(u[1], (W - W * q) % B, 1)
        turned_ref[q] = jnp.where(lane < W, first, jnp.where(lane < 2 * W, second, part))
    for s in range(NB):
        for a in range(NB):
            for q in range(B // W):
                dst = s * W + a * (B // W) + q
                if a <= s:
                    row = direct_ref[q, pl.ds(block(a, s), 1), :]
                else:
                    row = turned_ref[q, pl.ds(block(s, a), 1), :]
                out_ref[pl.ds(dst, 1), :] = row


def finish_kernel(all_rows, nz, got_ref, raw_ref, gram_ref, modes_ref):
    core = lax.axis_index("core")
    straight = lax.axis_index(SNAP) // (B // W) <= lax.axis_index(STATE)
    sums = []
    for c in range(2):
        total = got_ref[pl.ds(c, W, stride=2 * nz), :]
        for z in range(1, nz):
            total = total + got_ref[pl.ds(2 * z + c, W, stride=2 * nz), :]
        sums.append(total)
    direct = jnp.where(core == 0, sums[0], sums[1])
    whole = jnp.where(core == 0, sums[1], sums[0])[:1]
    turned = jnp.concatenate([sums[0], sums[1], sums[0], sums[1]], axis=0).T
    lane = lax.broadcasted_iota(jnp.int32, (W, B), 1)
    turned = jnp.where(lane < B // 2, turned[:W], turned[W : 2 * W])
    halves = jnp.where(lane[:1] < B // 2, pltpu.roll(sums[0][:1], B // 2, 1), sums[1][:1])
    gram_ref[...] = jnp.where(straight, direct, turned) / all_rows
    energy = jnp.where(straight, whole, halves)
    modes_ref[...] = raw_ref[...] * lax.rsqrt(energy / all_rows + 1e-06)


VMEM = pl.BlockSpec(memory_space=pltpu.VMEM)


def call(kernel, ins, outs, scratch, flops, moved):
    return pl.pallas_call(
        kernel,
        in_specs=[VMEM] * ins,
        out_specs=tuple(VMEM for _ in outs),
        out_shape=tuple(jax.ShapeDtypeStruct(shape, F32) for shape in outs),
        scratch_shapes=scratch,
        compiler_params=pltpu.CompilerParams(vmem_limit_bytes=40 << 20),
        cost_estimate=pl.CostEstimate(flops=flops, bytes_accessed=moved, transcendentals=0),
    )


def body(snapshots, coefficients):
    width, count = snapshots.shape
    nz, nc = lax.axis_size("zhi"), lax.axis_size("core")
    parts = lax.axis_size(SNAP)
    n = count // parts
    ns = width * parts
    all_rows = count * lax.axis_size(STATE)
    devices = lax.axis_size(ALL)
    rows = lax.all_to_all(snapshots, SNAP, split_axis=1, concat_axis=0, tiled=True)
    mine, other, raw = call(
        gram_kernel,
        2,
        [(W * CHUNK, B), (W * CHUNK, B), (n, B)],
        [pltpu.VMEM((ns, PAIR), F32)],
        2 * ns * n * (5 * ns // 8 + B),
        2 * ns * n + 8 * W * CHUNK * B + 4 * n * B,
    )(rows, coefficients)
    swap = [(i, 1 - i) for i in range(nc)]
    half = mine + lax.ppermute(other, "core", swap)
    got = lax.all_to_all(half.reshape(W, CHUNK, B), PLANE, 0, 0, tiled=True)
    (spread,) = call(
        spread_kernel,
        1,
        [(devices, B)],
        [pltpu.VMEM((B // W, HALF, B), F32)] * 2,
        W * CHUNK * B,
        4 * W * CHUNK * B,
    )(got)
    got = lax.all_to_all(spread.reshape(devices, 1, B), ALL, 0, 0, tiled=True)
    gram, modes = call(
        functools.partial(finish_kernel, all_rows, nz),
        2,
        [(W, B), (n, B)],
        [],
        n * B,
        8 * n * B,
    )(got.reshape(devices, B), raw)
    return (gram, modes)


def solution(mesh):
    fine = Mesh(mesh.devices.reshape(2, 4, 4, 4, 2), ALL)
    return jax.shard_map(
        body,
        mesh=fine,
        in_specs=(P(SNAP, STATE), P()),
        out_specs=(P(SNAP, STATE), P(STATE + SNAP, None)),
        check_vma=False,
    )
```

```python
import functools

import jax
import jax.numpy as jnp
from jax import lax
from jax.experimental import pallas as pl
from jax.experimental.pallas import tpu as pltpu
from jax.sharding import Mesh, PartitionSpec as P

ALL = ("zlo", "y", "x", "zhi", "core")
PLANE = ("x", "y", "zlo")
SPREAD = PLANE + ("zhi", "core")
SNAP = ("x", "zhi", "core")
STATE = ("zlo", "y")
B = 128
NB = 8
W = 32
BLOCKS = NB * (NB + 1) // 2
CHUNK = 2 * BLOCKS
PAIR = 2 * B
F32 = jnp.float32


def block(a, s):
    return s * (s + 1) // 2 + a


def target(s, a, q):
    p = a * (B // W) + q
    x, zhi, core = p // 8, p // 2 % 4, p % 2
    return (((x * 4 + s % 4) * 2 + s // 4) * 4 + zhi) * 2 + core


def low(shape):
    return lax.broadcasted_iota(jnp.int32, shape, 1) < B // 2


def gram_kernel(rows_ref, coef_ref, mine_ref, other_ref, raw_ref, tile_ref):
    core = lax.axis_index("core")
    raw_t = lax.dot_general(
        coef_ref[...], rows_ref[...], (((0,), (0,)), ((), ())), preferred_element_type=F32
    )
    raw = raw_t.T
    raw_ref[...] = raw
    energy = jnp.sum(raw * raw, axis=0, keepdims=True)
    energies = [energy, pltpu.roll(energy, B // 2, 1)]
    for sp in range(NB // 2):
        depth = (sp + 1) * PAIR
        tile_ref[:depth, :] = lax.dot_general(
            rows_ref[:depth, :],
            rows_ref[sp * PAIR : (sp + 1) * PAIR, :],
            (((1,), (1,)), ((), ())),
            preferred_element_type=F32,
        )
        for t in range(2):
            s = 2 * sp + t
            for a in range(s + 1):
                for slot in range(2):
                    top = a * B + slot * 2 * W
                    row = slot * BLOCKS + block(a, s)
                    for out_ref, c in ((mine_ref, core), (other_ref, 1 - core)):
                        part = tile_ref[
                            pl.ds(pl.multiple_of(top + c * W, W), W), t * B : (t + 1) * B
                        ]
                        if slot == 1 and a == s < 2:
                            part = jnp.where(low((W, B)), jnp.broadcast_to(energies[s], (W, B)), part)
                        out_ref[pl.ds(row, W, stride=CHUNK), :] = part


def spread_kernel(got_ref, out_ref, direct_ref, turned_ref, mixed_ref):
    core = lax.axis_index("core")
    chip = lax.axis_index(PLANE)
    total = got_ref[0]
    for i in range(1, W):
        total = total + got_ref[i]
    u = (total[:BLOCKS], total[BLOCKS:])
    first, second = (u[1][block(s, s) : block(s, s) + 1] for s in range(2))
    energy = jnp.where(low((1, B)), first, pltpu.roll(second, B // 2, 1))
    swapped = pltpu.roll(energy, B // 2, 1)
    shape = (BLOCKS, B)
    whole = jnp.broadcast_to(energy, shape)
    by_core = jnp.broadcast_to(jnp.where(core == 0, swapped, energy), shape)
    by_chip = jnp.broadcast_to(jnp.where(chip < W // 2, swapped, energy), shape)
    lane = lax.broadcasted_iota(jnp.int32, shape, 1)
    for q in range(B // W):
        own = core == q % 2
        direct_ref[q] = jnp.where(own, u[q // 2], whole)
        first = u[0] if q == 0 else pltpu.roll(u[0], B - W * q, 1)
        second = u[1] if q == 1 else pltpu.roll(u[1], (W - W * q) % B, 1)
        turned_ref[q] = jnp.where(lane < W, first, jnp.where(lane < 2 * W, second, by_core))
        mixed_ref[q] = jnp.where(lane < W, first, jnp.where(own, u[1], by_chip))
    for s in range(NB):
        for a in range(NB):
            for q in range(B // W):
                if a == s < 2 and q >= 2:
                    row = mixed_ref[q, pl.ds(block(a, s), 1), :]
                elif a <= s:
                    row = direct_ref[q, pl.ds(block(a, s), 1), :]
                else:
                    row = turned_ref[q, pl.ds(block(s, a), 1), :]
                out_ref[pl.ds(target(s, a, q), 1), :] = row


def finish_kernel(all_rows, nz, got_ref, raw_ref, gram_ref, modes_ref):
    place, stripe = lax.axis_index(SNAP), lax.axis_index(STATE)
    q, own_row = place % (B // W), place // (B // W)
    even = q % 2 == 0
    straight = own_row <= stripe
    mixed = jnp.logical_and(jnp.logical_and(own_row == stripe, stripe < 2), q >= 2)
    sums = []
    for c in range(2):
        total = got_ref[pl.ds(c, W, stride=2 * nz), :]
        for z in range(1, nz):
            total = total + got_ref[pl.ds(2 * z + c, W, stride=2 * nz), :]
        sums.append(total)
    direct = jnp.where(even, sums[0], sums[1])
    spare = jnp.where(even, sums[1], sums[0])
    flipped = jnp.concatenate([sums[0], sums[1], sums[0], sums[1]], axis=0).T
    left, one = low((W, B)), low((1, B))
    turned = jnp.where(left, flipped[:W], flipped[W : 2 * W])
    both = jnp.where(left, flipped[:W], direct)
    gram_ref[...] = jnp.where(straight, jnp.where(mixed, both, direct), turned) / all_rows
    by_core = jnp.where(one, pltpu.roll(sums[0][:1], B // 2, 1), sums[1][:1])
    by_chip = jnp.where(one, pltpu.roll(spare[:1], B // 2, 1), spare[W // 2 : W // 2 + 1])
    energy = jnp.where(straight, jnp.where(mixed, by_chip, spare[:1]), by_core)
    modes_ref[...] = raw_ref[...] * lax.rsqrt(energy / all_rows + 1e-06)


VMEM = pl.BlockSpec(memory_space=pltpu.VMEM)


def call(kernel, ins, outs, scratch, flops, moved):
    return pl.pallas_call(
        kernel,
        in_specs=[VMEM] * ins,
        out_specs=tuple(VMEM for _ in outs),
        out_shape=tuple(jax.ShapeDtypeStruct(shape, F32) for shape in outs),
        scratch_shapes=scratch,
        compiler_params=pltpu.CompilerParams(vmem_limit_bytes=40 << 20),
        cost_estimate=pl.CostEstimate(flops=flops, bytes_accessed=moved, transcendentals=0),
    )


def body(snapshots, coefficients):
    width, count = snapshots.shape
    nz, nc = lax.axis_size("zhi"), lax.axis_size("core")
    parts = lax.axis_size(SNAP)
    n = count // parts
    ns = width * parts
    all_rows = count * lax.axis_size(STATE)
    devices = lax.axis_size(ALL)
    rows = lax.all_to_all(snapshots, SNAP, split_axis=1, concat_axis=0, tiled=True)
    mine, other, raw = call(
        gram_kernel,
        2,
        [(W * CHUNK, B), (W * CHUNK, B), (n, B)],
        [pltpu.VMEM((ns, PAIR), F32)],
        2 * ns * n * (5 * ns // 8 + B),
        2 * ns * n + 8 * W * CHUNK * B + 4 * n * B,
    )(rows, coefficients)
    swap = [(i, 1 - i) for i in range(nc)]
    half = mine + lax.ppermute(other, "core", swap)
    got = lax.all_to_all(half.reshape(W, CHUNK, B), PLANE, 0, 0, tiled=True)
    (spread,) = call(
        spread_kernel,
        1,
        [(devices, B)],
        [pltpu.VMEM((B // W, BLOCKS, B), F32)] * 3,
        W * CHUNK * B,
        4 * W * CHUNK * B,
    )(got)
    got = lax.all_to_all(spread.reshape(devices, 1, B), SPREAD, 0, 0, tiled=True)
    gram, modes = call(
        functools.partial(finish_kernel, all_rows, nz),
        2,
        [(W, B), (n, B)],
        [],
        n * B,
        8 * n * B,
    )(got.reshape(devices, B), raw)
    return (gram, modes)


def solution(mesh):
    fine = Mesh(mesh.devices.reshape(2, 4, 4, 4, 2), ALL)
    return jax.shard_map(
        body,
        mesh=fine,
        in_specs=(P(SNAP, STATE), P()),
        out_specs=(P(SNAP, STATE), P(STATE + SNAP, None)),
        check_vma=False,
    )
```

```python
import functools

import jax
import jax.numpy as jnp
from jax import lax
from jax.experimental import pallas as pl
from jax.experimental.pallas import tpu as pltpu
from jax.sharding import Mesh, PartitionSpec as P

ALL = ("zlo", "y", "x", "zhi", "core")
PLANE = ("x", "y", "zlo")
SPREAD = PLANE + ("zhi", "core")
SNAP = ("x", "zhi", "core")
STATE = ("zlo", "y")
B = 128
NB = 8
W = 32
BLOCKS = NB * (NB + 1) // 2
CHUNK = 2 * BLOCKS
PAIR = 2 * B
F32 = jnp.float32


def block(a, s):
    return s * (s + 1) // 2 + a


def target(s, a, q):
    p = a * (B // W) + q
    x, zhi, core = p // 8, p // 2 % 4, p % 2
    return (((x * 4 + s % 4) * 2 + s // 4) * 4 + zhi) * 2 + core


def low(shape):
    return lax.broadcasted_iota(jnp.int32, shape, 1) < B // 2


def gram_kernel(rows_ref, mine_ref, other_ref, tile_ref):
    core = lax.axis_index("core")
    for sp in range(NB // 2):
        depth = (sp + 1) * PAIR
        tile_ref[:depth, :] = lax.dot_general(
            rows_ref[:depth, :],
            rows_ref[sp * PAIR : (sp + 1) * PAIR, :],
            (((1,), (1,)), ((), ())),
            preferred_element_type=F32,
        )
        for t in range(2):
            s = 2 * sp + t
            for a in range(s + 1):
                for slot in range(2):
                    top = a * B + slot * 2 * W
                    row = slot * BLOCKS + block(a, s)
                    for out_ref, c in ((mine_ref, core), (other_ref, 1 - core)):
                        part = tile_ref[
                            pl.ds(pl.multiple_of(top + c * W, W), W), t * B : (t + 1) * B
                        ]
                        out_ref[pl.ds(row, W, stride=CHUNK), :] = part


def raw_kernel(rows_ref, coef_ref, raw_ref, energy_ref):
    raw_t = lax.dot_general(
        coef_ref[...], rows_ref[...], (((0,), (0,)), ((), ())), preferred_element_type=F32
    )
    raw = raw_t.T
    raw_ref[...] = raw
    energy_ref[...] = jnp.sum(raw * raw, axis=0, keepdims=True)


def spread_kernel(got_ref, out_ref, direct_ref, turned_ref, mixed_ref):
    core = lax.axis_index("core")
    chip = lax.axis_index(PLANE)
    total = got_ref[0]
    for i in range(1, W):
        total = total + got_ref[i]
    u = (total[:BLOCKS], total[BLOCKS:])
    first, second = (u[1][block(s, s) : block(s, s) + 1] for s in range(2))
    energy = jnp.where(low((1, B)), first, pltpu.roll(second, B // 2, 1))
    swapped = pltpu.roll(energy, B // 2, 1)
    shape = (BLOCKS, B)
    whole = jnp.broadcast_to(energy, shape)
    by_core = jnp.broadcast_to(jnp.where(core == 0, swapped, energy), shape)
    by_chip = jnp.broadcast_to(jnp.where(chip < W // 2, swapped, energy), shape)
    lane = lax.broadcasted_iota(jnp.int32, shape, 1)
    for q in range(B // W):
        own = core == q % 2
        direct_ref[q] = jnp.where(own, u[q // 2], whole)
        first = u[0] if q == 0 else pltpu.roll(u[0], B - W * q, 1)
        second = u[1] if q == 1 else pltpu.roll(u[1], (W - W * q) % B, 1)
        turned_ref[q] = jnp.where(lane < W, first, jnp.where(lane < 2 * W, second, by_core))
        mixed_ref[q] = jnp.where(lane < W, first, jnp.where(own, u[1], by_chip))
    for s in range(NB):
        for a in range(NB):
            for q in range(B // W):
                if a == s < 2 and q >= 2:
                    row = mixed_ref[q, pl.ds(block(a, s), 1), :]
                elif a <= s:
                    row = direct_ref[q, pl.ds(block(a, s), 1), :]
                else:
                    row = turned_ref[q, pl.ds(block(s, a), 1), :]
                out_ref[pl.ds(target(s, a, q), 1), :] = row


def finish_kernel(all_rows, nz, got_ref, raw_ref, gram_ref, modes_ref):
    place, stripe = lax.axis_index(SNAP), lax.axis_index(STATE)
    q, own_row = place % (B // W), place // (B // W)
    even = q % 2 == 0
    straight = own_row <= stripe
    mixed = jnp.logical_and(jnp.logical_and(own_row == stripe, stripe < 2), q >= 2)
    sums = []
    for c in range(2):
        total = got_ref[pl.ds(c, W, stride=2 * nz), :]
        for z in range(1, nz):
            total = total + got_ref[pl.ds(2 * z + c, W, stride=2 * nz), :]
        sums.append(total)
    direct = jnp.where(even, sums[0], sums[1])
    spare = jnp.where(even, sums[1], sums[0])
    flipped = jnp.concatenate([sums[0], sums[1], sums[0], sums[1]], axis=0).T
    left, one = low((W, B)), low((1, B))
    turned = jnp.where(left, flipped[:W], flipped[W : 2 * W])
    both = jnp.where(left, flipped[:W], direct)
    gram_ref[...] = jnp.where(straight, jnp.where(mixed, both, direct), turned) / all_rows
    by_core = jnp.where(one, pltpu.roll(sums[0][:1], B // 2, 1), sums[1][:1])
    by_chip = jnp.where(one, pltpu.roll(spare[:1], B // 2, 1), spare[W // 2 : W // 2 + 1])
    energy = jnp.where(straight, jnp.where(mixed, by_chip, spare[:1]), by_core)
    modes_ref[...] = raw_ref[...] * lax.rsqrt(energy / all_rows + 1e-06)


VMEM = pl.BlockSpec(memory_space=pltpu.VMEM)


def call(kernel, ins, outs, scratch, flops, moved):
    return pl.pallas_call(
        kernel,
        in_specs=[VMEM] * ins,
        out_specs=tuple(VMEM for _ in outs),
        out_shape=tuple(jax.ShapeDtypeStruct(shape, F32) for shape in outs),
        scratch_shapes=scratch,
        compiler_params=pltpu.CompilerParams(vmem_limit_bytes=40 << 20),
        cost_estimate=pl.CostEstimate(flops=flops, bytes_accessed=moved, transcendentals=0),
    )


def body(snapshots, coefficients):
    width, count = snapshots.shape
    nz, nc = lax.axis_size("zhi"), lax.axis_size("core")
    parts = lax.axis_size(SNAP)
    n = count // parts
    ns = width * parts
    all_rows = count * lax.axis_size(STATE)
    devices = lax.axis_size(ALL)
    rows = lax.all_to_all(snapshots, SNAP, split_axis=1, concat_axis=0, tiled=True)
    mine, other = call(
        gram_kernel,
        1,
        [(W * CHUNK, B), (W * CHUNK, B)],
        [pltpu.VMEM((ns, PAIR), F32)],
        2 * ns * n * 5 * ns // 8,
        2 * ns * n + 8 * W * CHUNK * B,
    )(rows)
    swap = [(i, 1 - i) for i in range(nc)]
    got = lax.ppermute(other, "core", swap)
    raw, energy = call(
        raw_kernel, 2, [(n, B), (1, B)], [], 2 * ns * n * B, 2 * ns * n + 4 * n * B
    )(rows, coefficients)
    energy = energy + lax.ppermute(energy, "core", swap)
    place = lax.broadcasted_iota(jnp.int32, (1, CHUNK, B), 1) - BLOCKS
    left = lax.broadcasted_iota(jnp.int32, (1, CHUNK, B), 2) < B // 2
    turned = jnp.roll(energy, B // 2, 1)
    half = (mine + got).reshape(W, CHUNK, B)
    half = jnp.where(left & (place == block(0, 0)), energy[None], half)
    half = jnp.where(left & (place == block(1, 1)), turned[None], half)
    got = lax.all_to_all(half, PLANE, 0, 0, tiled=True)
    (spread,) = call(
        spread_kernel,
        1,
        [(devices, B)],
        [pltpu.VMEM((B // W, BLOCKS, B), F32)] * 3,
        W * CHUNK * B,
        4 * W * CHUNK * B,
    )(got)
    got = lax.all_to_all(spread.reshape(devices, 1, B), SPREAD, 0, 0, tiled=True)
    gram, modes = call(
        functools.partial(finish_kernel, all_rows, nz),
        2,
        [(W, B), (n, B)],
        [],
        n * B,
        8 * n * B,
    )(got.reshape(devices, B), raw)
    return (gram, modes)


def solution(mesh):
    fine = Mesh(mesh.devices.reshape(2, 4, 4, 4, 2), ALL)
    return jax.shard_map(
        body,
        mesh=fine,
        in_specs=(P(SNAP, STATE), P()),
        out_specs=(P(SNAP, STATE), P(STATE + SNAP, None)),
        check_vma=False,
    )
```

```python
import functools

import jax
import jax.numpy as jnp
from jax import lax
from jax.experimental import pallas as pl
from jax.experimental.pallas import tpu as pltpu
from jax.sharding import Mesh, PartitionSpec as P

ALL = ("zlo", "y", "x", "zhi", "core")
PLANE = ("x", "y", "zlo")
SPREAD = PLANE + ("zhi", "core")
SNAP = ("x", "zhi", "core")
STATE = ("zlo", "y")
B = 128
NB = 8
W = 32
BLOCKS = NB * (NB + 1) // 2
CHUNK = 2 * BLOCKS
PAIR = 2 * B
F32 = jnp.float32


def block(a, s):
    return s * (s + 1) // 2 + a


def target(s, a, q):
    p = a * (B // W) + q
    x, zhi, core = p // 8, p // 2 % 4, p % 2
    return (((x * 4 + s % 4) * 2 + s // 4) * 4 + zhi) * 2 + core


def low(shape):
    return lax.broadcasted_iota(jnp.int32, shape, 1) < B // 2


def gram_kernel(own, rows_ref, out_ref, tile_ref, left_ref):
    core = lax.axis_index("core")
    first = (core if own else 1 - core) * W
    for i in range(NB * 2):
        left_ref[i * W : (i + 1) * W, :] = rows_ref[pl.ds(pl.multiple_of(2 * i * W + first, W), W), :]
    for sp in range(NB // 2):
        depth = (sp + 1) * B
        tile_ref[:depth, :] = lax.dot_general(
            left_ref[:depth, :],
            rows_ref[sp * PAIR : (sp + 1) * PAIR, :],
            (((1,), (1,)), ((), ())),
            preferred_element_type=F32,
        )
        for t in range(2):
            s = 2 * sp + t
            for a in range(s + 1):
                for slot in range(2):
                    row = slot * BLOCKS + block(a, s)
                    top = (2 * a + slot) * W
                    out_ref[pl.ds(row, W, stride=CHUNK), :] = tile_ref[
                        top : top + W, t * B : (t + 1) * B
                    ]


def raw_kernel(rows_ref, coef_ref, raw_ref, energy_ref):
    raw_t = lax.dot_general(
        coef_ref[...], rows_ref[...], (((0,), (0,)), ((), ())), preferred_element_type=F32
    )
    raw = raw_t.T
    raw_ref[...] = raw
    energy_ref[...] = jnp.sum(raw * raw, axis=0, keepdims=True)


def spread_kernel(got_ref, out_ref, direct_ref, turned_ref, mixed_ref):
    core = lax.axis_index("core")
    chip = lax.axis_index(PLANE)
    total = got_ref[0]
    for i in range(1, W):
        total = total + got_ref[i]
    u = (total[:BLOCKS], total[BLOCKS:])
    first, second = (u[1][block(s, s) : block(s, s) + 1] for s in range(2))
    energy = jnp.where(low((1, B)), first, pltpu.roll(second, B // 2, 1))
    swapped = pltpu.roll(energy, B // 2, 1)
    shape = (BLOCKS, B)
    whole = jnp.broadcast_to(energy, shape)
    by_core = jnp.broadcast_to(jnp.where(core == 0, swapped, energy), shape)
    by_chip = jnp.broadcast_to(jnp.where(chip < W // 2, swapped, energy), shape)
    lane = lax.broadcasted_iota(jnp.int32, shape, 1)
    for q in range(B // W):
        own = core == q % 2
        direct_ref[q] = jnp.where(own, u[q // 2], whole)
        first = u[0] if q == 0 else pltpu.roll(u[0], B - W * q, 1)
        second = u[1] if q == 1 else pltpu.roll(u[1], (W - W * q) % B, 1)
        turned_ref[q] = jnp.where(lane < W, first, jnp.where(lane < 2 * W, second, by_core))
        mixed_ref[q] = jnp.where(lane < W, first, jnp.where(own, u[1], by_chip))
    for s in range(NB):
        for a in range(NB):
            for q in range(B // W):
                if a == s < 2 and q >= 2:
                    row = mixed_ref[q, pl.ds(block(a, s), 1), :]
                elif a <= s:
                    row = direct_ref[q, pl.ds(block(a, s), 1), :]
                else:
                    row = turned_ref[q, pl.ds(block(s, a), 1), :]
                out_ref[pl.ds(target(s, a, q), 1), :] = row


def finish_kernel(all_rows, nz, got_ref, raw_ref, gram_ref, modes_ref):
    place, stripe = lax.axis_index(SNAP), lax.axis_index(STATE)
    q, own_row = place % (B // W), place // (B // W)
    even = q % 2 == 0
    straight = own_row <= stripe
    mixed = jnp.logical_and(jnp.logical_and(own_row == stripe, stripe < 2), q >= 2)
    sums = []
    for c in range(2):
        total = got_ref[pl.ds(c, W, stride=2 * nz), :]
        for z in range(1, nz):
            total = total + got_ref[pl.ds(2 * z + c, W, stride=2 * nz), :]
        sums.append(total)
    direct = jnp.where(even, sums[0], sums[1])
    spare = jnp.where(even, sums[1], sums[0])
    flipped = jnp.concatenate([sums[0], sums[1], sums[0], sums[1]], axis=0).T
    left, one = low((W, B)), low((1, B))
    turned = jnp.where(left, flipped[:W], flipped[W : 2 * W])
    both = jnp.where(left, flipped[:W], direct)
    gram_ref[...] = jnp.where(straight, jnp.where(mixed, both, direct), turned) / all_rows
    by_core = jnp.where(one, pltpu.roll(sums[0][:1], B // 2, 1), sums[1][:1])
    by_chip = jnp.where(one, pltpu.roll(spare[:1], B // 2, 1), spare[W // 2 : W // 2 + 1])
    energy = jnp.where(straight, jnp.where(mixed, by_chip, spare[:1]), by_core)
    modes_ref[...] = raw_ref[...] * lax.rsqrt(energy / all_rows + 1e-06)


VMEM = pl.BlockSpec(memory_space=pltpu.VMEM)


def call(kernel, ins, outs, scratch, flops, moved):
    return pl.pallas_call(
        kernel,
        in_specs=[VMEM] * ins,
        out_specs=tuple(VMEM for _ in outs),
        out_shape=tuple(jax.ShapeDtypeStruct(shape, F32) for shape in outs),
        scratch_shapes=scratch,
        compiler_params=pltpu.CompilerParams(vmem_limit_bytes=40 << 20),
        cost_estimate=pl.CostEstimate(flops=flops, bytes_accessed=moved, transcendentals=0),
    )


def body(snapshots, coefficients):
    width, count = snapshots.shape
    nz, nc = lax.axis_size("zhi"), lax.axis_size("core")
    parts = lax.axis_size(SNAP)
    n = count // parts
    ns = width * parts
    all_rows = count * lax.axis_size(STATE)
    devices = lax.axis_size(ALL)
    rows = lax.all_to_all(snapshots, SNAP, split_axis=1, concat_axis=0, tiled=True)
    halves = [
        call(
            functools.partial(gram_kernel, own),
            1,
            [(W * CHUNK, B)],
            [pltpu.VMEM((ns // 2, PAIR), F32), pltpu.VMEM((ns // 2, n), rows.dtype)],
            ns * n * 5 * ns // 8,
            2 * ns * n + 4 * W * CHUNK * B,
        )
        for own in (False, True)
    ]
    swap = [(i, 1 - i) for i in range(nc)]
    (other,) = halves[0](rows)
    got = lax.ppermute(other, "core", swap)
    raw, energy = call(
        raw_kernel, 2, [(n, B), (1, B)], [], 2 * ns * n * B, 2 * ns * n + 4 * n * B
    )(rows, coefficients)
    (mine,) = halves[1](rows)
    energy = energy + lax.ppermute(energy, "core", swap)
    place = lax.broadcasted_iota(jnp.int32, (1, CHUNK, B), 1) - BLOCKS
    left = lax.broadcasted_iota(jnp.int32, (1, CHUNK, B), 2) < B // 2
    turned = jnp.roll(energy, B // 2, 1)
    half = (mine + got).reshape(W, CHUNK, B)
    half = jnp.where(left & (place == block(0, 0)), energy[None], half)
    half = jnp.where(left & (place == block(1, 1)), turned[None], half)
    got = lax.all_to_all(half, PLANE, 0, 0, tiled=True)
    (spread,) = call(
        spread_kernel,
        1,
        [(devices, B)],
        [pltpu.VMEM((B // W, BLOCKS, B), F32)] * 3,
        W * CHUNK * B,
        4 * W * CHUNK * B,
    )(got)
    got = lax.all_to_all(spread.reshape(devices, 1, B), SPREAD, 0, 0, tiled=True)
    gram, modes = call(
        functools.partial(finish_kernel, all_rows, nz),
        2,
        [(W, B), (n, B)],
        [],
        n * B,
        8 * n * B,
    )(got.reshape(devices, B), raw)
    return (gram, modes)


def solution(mesh):
    fine = Mesh(mesh.devices.reshape(2, 4, 4, 4, 2), ALL)
    return jax.shard_map(
        body,
        mesh=fine,
        in_specs=(P(SNAP, STATE), P()),
        out_specs=(P(SNAP, STATE), P(STATE + SNAP, None)),
        check_vma=False,
    )
```

```python
import functools

import jax
import jax.numpy as jnp
from jax import lax
from jax.experimental import pallas as pl
from jax.experimental.pallas import tpu as pltpu
from jax.sharding import Mesh, PartitionSpec as P

ALL = ("zlo", "y", "x", "zhi", "core")
PLANE = ("x", "y", "zlo")
SPREAD = PLANE + ("zhi", "core")
SNAP = ("x", "zhi", "core")
STATE = ("zlo", "y")
B = 128
NB = 8
W = 32
BLOCKS = NB * (NB + 1) // 2
CHUNK = 2 * BLOCKS
PAIR = 2 * B
F32 = jnp.float32


def block(a, s):
    return s * (s + 1) // 2 + a


def target(s, a, q):
    p = a * (B // W) + q
    x, zhi, core = p // 8, p // 2 % 4, p % 2
    return (((x * 4 + s % 4) * 2 + s // 4) * 4 + zhi) * 2 + core


def low(shape):
    return lax.broadcasted_iota(jnp.int32, shape, 1) < B // 2


def gram_kernel(own, rows_ref, out_ref, tile_ref, left_ref):
    core = lax.axis_index("core")
    first = (core if own else 1 - core) * W
    for i in range(NB * 2):
        left_ref[i * W : (i + 1) * W, :] = rows_ref[pl.ds(pl.multiple_of(2 * i * W + first, W), W), :]
    for sp in range(NB // 2):
        depth = (sp + 1) * B
        tile_ref[:depth, :] = lax.dot_general(
            left_ref[:depth, :],
            rows_ref[sp * PAIR : (sp + 1) * PAIR, :],
            (((1,), (1,)), ((), ())),
            preferred_element_type=F32,
        )
        for t in range(2):
            s = 2 * sp + t
            for a in range(s + 1):
                for slot in range(2):
                    row = slot * BLOCKS + block(a, s)
                    top = (2 * a + slot) * W
                    out_ref[pl.ds(row, W, stride=CHUNK), :] = tile_ref[
                        top : top + W, t * B : (t + 1) * B
                    ]


def raw_kernel(rows_ref, coef_ref, raw_ref, energy_ref):
    raw_t = lax.dot_general(
        coef_ref[...], rows_ref[...], (((0,), (0,)), ((), ())), preferred_element_type=F32
    )
    raw = raw_t.T
    raw_ref[...] = raw
    energy_ref[...] = jnp.sum(raw * raw, axis=0, keepdims=True)


def spread_kernel(got_ref, out_ref, direct_ref, turned_ref, mixed_ref):
    core = lax.axis_index("core")
    chip = lax.axis_index(PLANE)
    total = got_ref[0]
    for i in range(1, W):
        total = total + got_ref[i]
    u = (total[:BLOCKS], total[BLOCKS:])
    first, second = (u[1][block(s, s) : block(s, s) + 1] for s in range(2))
    energy = jnp.where(low((1, B)), first, pltpu.roll(second, B // 2, 1))
    swapped = pltpu.roll(energy, B // 2, 1)
    shape = (BLOCKS, B)
    whole = jnp.broadcast_to(energy, shape)
    by_core = jnp.broadcast_to(jnp.where(core == 0, swapped, energy), shape)
    by_chip = jnp.broadcast_to(jnp.where(chip < W // 2, swapped, energy), shape)
    lane = lax.broadcasted_iota(jnp.int32, shape, 1)
    for q in range(B // W):
        own = core == q % 2
        direct_ref[q] = jnp.where(own, u[q // 2], whole)
        first = u[0] if q == 0 else pltpu.roll(u[0], B - W * q, 1)
        second = u[1] if q == 1 else pltpu.roll(u[1], (W - W * q) % B, 1)
        turned_ref[q] = jnp.where(lane < W, first, jnp.where(lane < 2 * W, second, by_core))
        mixed_ref[q] = jnp.where(lane < W, first, jnp.where(own, u[1], by_chip))
    for s in range(NB):
        for a in range(NB):
            for q in range(B // W):
                if a == s < 2 and q >= 2:
                    row = mixed_ref[q, pl.ds(block(a, s), 1), :]
                elif a <= s:
                    row = direct_ref[q, pl.ds(block(a, s), 1), :]
                else:
                    row = turned_ref[q, pl.ds(block(s, a), 1), :]
                out_ref[pl.ds(target(s, a, q), 1), :] = row


def finish_kernel(all_rows, nz, got_ref, raw_ref, gram_ref, modes_ref):
    place, stripe = lax.axis_index(SNAP), lax.axis_index(STATE)
    q, own_row = place % (B // W), place // (B // W)
    even = q % 2 == 0
    straight = own_row <= stripe
    mixed = jnp.logical_and(jnp.logical_and(own_row == stripe, stripe < 2), q >= 2)
    sums = []
    for c in range(2):
        total = got_ref[pl.ds(c, W, stride=2 * nz), :]
        for z in range(1, nz):
            total = total + got_ref[pl.ds(2 * z + c, W, stride=2 * nz), :]
        sums.append(total)
    direct = jnp.where(even, sums[0], sums[1])
    spare = jnp.where(even, sums[1], sums[0])
    flipped = jnp.concatenate([sums[0], sums[1], sums[0], sums[1]], axis=0).T
    left, one = low((W, B)), low((1, B))
    turned = jnp.where(left, flipped[:W], flipped[W : 2 * W])
    both = jnp.where(left, flipped[:W], direct)
    gram_ref[...] = jnp.where(straight, jnp.where(mixed, both, direct), turned) / all_rows
    by_core = jnp.where(one, pltpu.roll(sums[0][:1], B // 2, 1), sums[1][:1])
    by_chip = jnp.where(one, pltpu.roll(spare[:1], B // 2, 1), spare[W // 2 : W // 2 + 1])
    energy = jnp.where(straight, jnp.where(mixed, by_chip, spare[:1]), by_core)
    modes_ref[...] = raw_ref[...] * lax.rsqrt(energy / all_rows + 1e-06)


VMEM = pl.BlockSpec(memory_space=pltpu.VMEM)


def call(kernel, ins, outs, scratch, flops, moved):
    return pl.pallas_call(
        kernel,
        in_specs=[VMEM] * ins,
        out_specs=tuple(VMEM for _ in outs),
        out_shape=tuple(jax.ShapeDtypeStruct(shape, F32) for shape in outs),
        scratch_shapes=scratch,
        compiler_params=pltpu.CompilerParams(vmem_limit_bytes=40 << 20),
        cost_estimate=pl.CostEstimate(flops=flops, bytes_accessed=moved, transcendentals=0),
    )


def body(snapshots, coefficients):
    width, count = snapshots.shape
    nz, nc = lax.axis_size("zhi"), lax.axis_size("core")
    parts = lax.axis_size(SNAP)
    n = count // parts
    ns = width * parts
    all_rows = count * lax.axis_size(STATE)
    devices = lax.axis_size(ALL)
    rows = lax.all_to_all(snapshots, SNAP, split_axis=1, concat_axis=0, tiled=True)
    halves = [
        call(
            functools.partial(gram_kernel, own),
            1,
            [(W * CHUNK, B)],
            [pltpu.VMEM((ns // 2, PAIR), F32), pltpu.VMEM((ns // 2, n), rows.dtype)],
            ns * n * 5 * ns // 8,
            2 * ns * n + 4 * W * CHUNK * B,
        )
        for own in (False, True)
    ]
    swap = [(i, 1 - i) for i in range(nc)]
    (other,) = halves[0](rows)
    got = lax.ppermute(other, "core", swap)
    raw, energy = call(
        raw_kernel, 2, [(n, B), (1, B)], [], 2 * ns * n * B, 2 * ns * n + 4 * n * B
    )(rows, coefficients)
    (mine,) = halves[1](rows)
    energy = energy + lax.ppermute(energy, "core", swap)
    place = lax.broadcasted_iota(jnp.int32, (1, CHUNK, B), 1) - BLOCKS
    left = lax.broadcasted_iota(jnp.int32, (1, CHUNK, B), 2) < B // 2
    turned = jnp.roll(energy, B // 2, 1)
    half = mine.reshape(W, CHUNK, B) + got.reshape(W, CHUNK, B)
    half = jnp.where(left & (place == block(0, 0)), energy[None], half)
    half = jnp.where(left & (place == block(1, 1)), turned[None], half)
    got = lax.all_to_all(half, PLANE, 0, 0, tiled=True)
    (spread,) = call(
        spread_kernel,
        1,
        [(devices, B)],
        [pltpu.VMEM((B // W, BLOCKS, B), F32)] * 3,
        W * CHUNK * B,
        4 * W * CHUNK * B,
    )(got)
    got = lax.all_to_all(spread.reshape(devices, 1, B), SPREAD, 0, 0, tiled=True)
    gram, modes = call(
        functools.partial(finish_kernel, all_rows, nz),
        2,
        [(W, B), (n, B)],
        [],
        n * B,
        8 * n * B,
    )(got.reshape(devices, B), raw)
    return (gram, modes)


def solution(mesh):
    fine = Mesh(mesh.devices.reshape(2, 4, 4, 4, 2), ALL)
    return jax.shard_map(
        body,
        mesh=fine,
        in_specs=(P(SNAP, STATE), P()),
        out_specs=(P(SNAP, STATE), P(STATE + SNAP, None)),
        check_vma=False,
    )
```
